256 devices in a mesh: grp: 2 (over core), row: 4 (over x), col: 32 (over z, y).
Axes of the slice: x: 4, y: 4, z: 8, core: 2. Of those that a mesh axis runs over, the one named last changes fastest.
Arguments:
- resid: bfloat16 [512, 5120], P(('grp', 'col'), 'row'), may hold values from -6 to 6
- query: bfloat16 [128, 4, 4096], P(('row', 'col'), None, 'grp'), may hold values from -11 to 11
- key_new: bfloat16 [128, 4, 1024], P(('row', 'col'), None, 'grp'), may hold values from -6 to 6
- value_new: bfloat16 [128, 4, 1024], P(('row', 'col'), None, 'grp'), may hold values from -6 to 6
- key_cache: bfloat16 [128, 2048, 1024], P(('row', 'col'), None, 'grp'), may hold values from -11 to 11
- value_cache: bfloat16 [128, 2048, 1024], P(('row', 'col'), None, 'grp'), may hold values from -6 to 6
- ctx_len: int32 [128], P(('row', 'col')), may hold values from 512 to 2048, as said below
- ssm_x: bfloat16 [128, 4, 8192], P(('row', 'col'), None, 'grp'), may hold values from -6 to 6
- ssm_gate: bfloat16 [128, 4, 8192], P(('row', 'col'), None, 'grp'), may hold values from -6 to 6
- ssm_b: bfloat16 [128, 4, 128], P(('row', 'col')), may hold values from -6 to 6
- ssm_c: bfloat16 [128, 4, 128], P(('row', 'col')), may hold values from -0.59765625 to 0.59765625
- ssm_dt: float32 [128, 4, 64], P(('row', 'col'), None, 'grp'), may hold values from 0.02 to 1
- decay_rate: float32 [64], P('grp'), may hold values from 0.05 to 8
- skip_gain: float32 [64], P('grp'), may hold values from 0.5 to 1.5
- ssm_state: float32 [128, 64, 128, 128], P(('row', 'col'), 'grp'), may hold values from -2 to 2
- accepted: int32 [128], P(('row', 'col')), may hold values from 0 to 4
- slot_of: int32 [128], replicated, may hold values from 0 to 127, each once
- w_out: bfloat16 [12288, 5120], P(('grp', 'col'), 'row'), may hold values from -0.0546875 to 0.0546875
- norm_gain: float32 [5120], P('row'), may hold values from 0.5 to 1.5
- gate_up: bfloat16 [5120, 2, 21504], P('row', None, ('grp', 'col')), may hold values from -0.078125 to 0.078125
- w_down: bfloat16 [21504, 5120], P(('grp', 'col'), 'row'), may hold values from -0.0390625 to 0.0390625
Outputs:
- layer_out: bfloat16 [512, 5120], P(('grp', 'col'), 'row')
- state_next: float32 [128, 64, 128, 128], P(('row', 'col'), 'grp')
The draws below stay inside these ranges and needn't reach their ends.
Inputs may be any that keep to these rules, and one draw needn't show every extreme that they name: `ctx_len`: cache entries at positions at or past a slot's length are not part of its context; some slot has length 2048. `slot_of`: each slot holds exactly one request.
All inputs are finite; a program needn't handle non-finite values.
Results may differ from the reference program's by a relative error of at most 0.0052.
Values may be sent and summed in bfloat16 or wider, within the bound.
No kernel may reach another device: no remote copies, remote signals or barrier semaphores. Data moves between devices by JAX's collectives and lax.ppermute only.
A program may use at most 64 MiB of HBM per device.

```python
import math
import jax
import jax.numpy as jnp
from jax import lax

D = 5120
FF = 21504
HQ = 32
HK = 8
HD = 128
HS = 64
PH = 128
NS = 128
Q = 4
CTX = 2048
REQS = 128
TOK = 512
F = 12288


def draw_ctx_len(key, part):
    key = jax.random.fold_in(key, 11)
    lengths = jax.random.randint(key, (REQS,), CTX // 4, CTX + 1)
    return lengths.at[0].set(CTX).astype(jnp.int32)


def shared_parts(key):
    shuffled = jax.random.permutation(jax.random.fold_in(key, 1), REQS)
    picked = shuffled < max(1, REQS // 4)
    target = jnp.exp(jax.random.uniform(jax.random.fold_in(key, 2), (REQS,), jnp.float32, math.log(120.0), math.log(420.0)))
    sign_rows = jnp.where(jax.random.bernoulli(jax.random.fold_in(key, 3), 0.5, (REQS, HK, HD)), 1.0, -1.0).astype(jnp.float32)
    first_pos = jax.random.randint(jax.random.fold_in(key, 4), (REQS,), 0, max(1, CTX // 8))
    second_pos = CTX // 8 + jax.random.randint(jax.random.fold_in(key, 5), (REQS,), 0, max(1, CTX // 8))
    score_gap = jax.random.uniform(jax.random.fold_in(key, 6), (REQS,), jnp.float32, 1.0, 3.0)
    magnitude = jnp.sqrt(target / math.sqrt(HD))
    return (picked, sign_rows, first_pos, second_pos, score_gap, magnitude)


def drawn_part(key, shape):
    return jnp.clip(jax.random.normal(key, shape, jnp.float32), -6.0, 6.0)


def draw_query(key, part):
    picked, sign_rows, first_pos, second_pos, score_gap, magnitude = shared_parts(key)
    key = jax.random.fold_in(key, 21)
    drawn = drawn_part(key, (REQS, Q, HQ * HD))
    aligned = jnp.repeat(sign_rows, HQ // HK, axis=1) * magnitude[:, None, None]
    aligned = aligned.reshape(REQS, 1, HQ * HD)
    return jnp.where(picked[:, None, None], aligned, drawn).astype(jnp.bfloat16)


def draw_key_cache(key, part):
    picked, sign_rows, first_pos, second_pos, score_gap, magnitude = shared_parts(key)
    key = jax.random.fold_in(key, 22)
    drawn = drawn_part(key, (REQS, CTX, HK * HD))
    key_row = sign_rows * magnitude[:, None, None]
    lowered = sign_rows * (magnitude - score_gap * math.sqrt(HD) / magnitude)[:, None, None]
    head_start = (jnp.arange(HD) == 0)[None, None, :]
    second_row = jnp.where(head_start, lowered, key_row).reshape(REQS, HK * HD)
    key_row = key_row.reshape(REQS, HK * HD)
    position = jnp.arange(CTX)[None, :]
    at_first = (position == first_pos[:, None]) & picked[:, None]
    at_second = (position == second_pos[:, None]) & picked[:, None]
    result = jnp.where(at_first[:, :, None], key_row[:, None, :], drawn)
    return jnp.where(at_second[:, :, None], second_row[:, None, :], result).astype(jnp.bfloat16)


def set_ends(values, stream_key, least, largest):
    extent = values.shape
    place = [jax.random.randint(jax.random.fold_in(stream_key, axis), (), 0, extent[axis]) for axis in range(len(extent))]
    values = values.at[tuple(place)].set(least)
    longest = extent.index(max(extent))
    place[longest] = (place[longest] + 1) % extent[longest]
    return values.at[tuple(place)].set(largest)


def shard_levels(own_key, dims, pieces, least, high):
    def one(axis_at, blocks):
        steps = jax.random.uniform(jax.random.fold_in(jax.random.fold_in(own_key, 6), axis_at), (blocks,), jnp.float32, least / len(pieces), high / len(pieces))
        return jnp.repeat(jnp.exp(steps), dims[axis_at] // blocks).reshape((-1,) + (1,) * (len(dims) - axis_at - 1))

    factor_of = one(*pieces[0])
    for cut in pieces[1:]:
        factor_of = factor_of * one(*cut)
    return factor_of


def centred(key, extent, width, bound, cuts=(), kind=jnp.bfloat16):
    factor_of = shard_levels(key, extent, cuts, -0.22, 0.18) if cuts else 1.0
    entries = jax.random.normal(key, extent, jnp.float32) * width * factor_of
    return jnp.minimum(jnp.maximum(entries, -bound), bound).astype(kind)


def setup_inputs(seed: int = 0) -> dict:
    seeds = jax.random.split(jax.random.key(seed), 22)
    return {
        "resid": centred(seeds[0], (TOK, D), 1.0, 6.0, ((0, 64), (1, 4))),
        "query": draw_query(jax.random.fold_in(seeds[21], 71), 0),
        "key_new": centred(seeds[2], (REQS, Q, HK * HD), 1.0, 6.0, ((0, 128), (2, 2))),
        "value_new": centred(seeds[3], (REQS, Q, HK * HD), 1.0, 6.0, ((0, 128), (2, 2))),
        "key_cache": draw_key_cache(jax.random.fold_in(seeds[21], 71), 0),
        "value_cache": centred(seeds[5], (REQS, CTX, HK * HD), 1.0, 6.0, ((0, 128), (2, 2))),
        "ctx_len": draw_ctx_len(jax.random.fold_in(seeds[21], 71), 0),
        "ssm_x": centred(seeds[7], (REQS, Q, HS * PH), 1.0, 6.0, ((0, 128), (2, 2))),
        "ssm_gate": centred(seeds[8], (REQS, Q, HS * PH), 1.0, 6.0, ((0, 128), (2, 2))),
        "ssm_b": centred(seeds[9], (REQS, Q, NS), 1.0, 6.0, ((0, 128),)),
        "ssm_c": centred(seeds[10], (REQS, Q, NS), 0.1, 0.59765625, ((0, 128),)),
        "ssm_dt": jnp.clip(jnp.exp(math.log(1.0) - 3.912023 * jax.random.uniform(seeds[11], (REQS, Q, HS), jnp.float32) ** shard_levels(seeds[11], (REQS, Q, HS), ((0, 128), (2, 2)), -0.2, 0.2)), 0.02, 1.0),
        "decay_rate": jnp.clip(jnp.exp(math.log(8.0) - 5.075174 * jax.random.uniform(seeds[12], (HS,), jnp.float32) ** shard_levels(seeds[12], (HS,), ((0, 2),), -0.2, 0.2)), 0.05, 8.0),
        "skip_gain": jnp.clip(0.5 + 1.0 * jax.random.uniform(seeds[13], (HS,), jnp.float32) ** shard_levels(seeds[13], (HS,), ((0, 2),), -0.2, 0.2), 0.5, 1.5),
        "ssm_state": centred(seeds[14], (REQS, HS, PH, NS), 0.3, 2.0, ((0, 128), (1, 2)), jnp.float32),
        "accepted": set_ends(jax.random.randint(seeds[15], (REQS,), 0, Q + 1), jax.random.fold_in(seeds[15], 1), 0, Q).astype(jnp.int32),
        "slot_of": jax.random.permutation(seeds[16], REQS).astype(jnp.int32),
        "w_out": centred(seeds[17], (F, D), F ** -0.5, 0.0546875, ((0, 64), (1, 4))),
        "norm_gain": jnp.clip(1.0 + 0.1 * jax.random.normal(seeds[18], (D,), jnp.float32), 0.5, 1.5),
        "gate_up": centred(seeds[19], (D, 2, FF), D ** -0.5, 0.078125, ((0, 4), (2, 64))),
        "w_down": centred(seeds[20], (FF, D), FF ** -0.5, 0.0390625, ((0, 64), (1, 4))),
    }


norm_eps = 1e-05

def visible(length, cache_len, steps_new):
    position = jnp.arange(cache_len + steps_new)[None, :]
    drafts = jnp.arange(steps_new)[:, None]
    return jnp.where(position < cache_len, position < length, position - cache_len <= drafts)

def attend_whole(request):
    queries, keys_new, values_new, keys_cache, values_cache, length = request
    steps_new = queries.shape[0]
    kv_heads = keys_new.shape[1] // HD
    groups = queries.shape[1] // keys_new.shape[1]
    q_heads = queries.astype(jnp.float32).reshape(steps_new, kv_heads, groups, HD)
    keys_all = jnp.concatenate([keys_cache, keys_new], 0).astype(jnp.float32).reshape(-1, kv_heads, HD)
    values_all = jnp.concatenate([values_cache, values_new], 0).astype(jnp.float32).reshape(-1, kv_heads, HD)
    scores = jnp.einsum('qjgd,kjd->jgqk', q_heads, keys_all) * HD ** (-0.5)
    live = visible(length, keys_cache.shape[0], steps_new)
    scores = jnp.where(live[None, None], scores, -jnp.inf)
    peak = lax.optimization_barrier(jnp.max(scores, axis=-1, keepdims=True))
    weights = jnp.exp(scores - peak)
    total = lax.optimization_barrier(jnp.sum(weights, axis=-1))
    rounded = weights.astype(jnp.bfloat16).astype(jnp.float32)
    summed = jnp.einsum('jgqk,kjd->qjgd', rounded, values_all)
    result = summed / jnp.transpose(total, (2, 0, 1))[..., None]
    return result.reshape(steps_new, -1).astype(jnp.bfloat16)

def ssm_scan(ssm_x, ssm_gate, ssm_b, ssm_c, ssm_dt, decay_rate, skip_gain, ssm_state, accepted):
    count = ssm_x.shape[0]
    steps_new = ssm_x.shape[1]
    heads = decay_rate.shape[0]
    inputs = ssm_x.astype(jnp.float32).reshape(count, steps_new, heads, PH)
    in_map = ssm_b.astype(jnp.float32)
    out_map = ssm_c.astype(jnp.float32)
    state = ssm_state
    kept = ssm_state
    outputs = []
    for t in range(steps_new):
        decay = jnp.exp(-ssm_dt[:, t, :] * decay_rate[None, :])
        driven = ssm_dt[:, t, :, None] * inputs[:, t]
        state = decay[:, :, None, None] * state + driven[:, :, :, None] * in_map[:, t, None, None, :]
        readout = jnp.einsum('rhpn,rn->rhp', state, out_map[:, t], precision=lax.Precision.HIGHEST)
        outputs.append(readout + skip_gain[None, :, None] * inputs[:, t])
        kept = jnp.where((accepted > t)[:, None, None, None], state, kept)
    stacked = jnp.stack(outputs, axis=1).reshape(count, steps_new, heads * PH)
    gated = stacked * jax.nn.silu(ssm_gate.astype(jnp.float32))
    return (gated.astype(jnp.bfloat16), kept)

def reference(resid, query, key_new, value_new, key_cache, value_cache, ctx_len, ssm_x, ssm_gate, ssm_b, ssm_c, ssm_dt, decay_rate, skip_gain, ssm_state, accepted, slot_of, w_out, norm_gain, gate_up, w_down):
    attended = lax.map(attend_whole, (query, key_new, value_new, key_cache, value_cache, ctx_len))
    ssm_out, state_next = ssm_scan(ssm_x, ssm_gate, ssm_b, ssm_c, ssm_dt, decay_rate, skip_gain, ssm_state, accepted)
    half_attn = HQ * HD // 2
    half_ssm = HS * PH // 2
    mixed = jnp.concatenate([attended[..., :half_attn], ssm_out[..., :half_ssm], attended[..., half_attn:], ssm_out[..., half_ssm:]], axis=-1)
    mixed_req = jnp.take(mixed, slot_of, axis=0).reshape(TOK, -1)
    stream = resid.astype(jnp.float32) + jnp.dot(mixed_req, w_out, preferred_element_type=jnp.float32)
    mean_sq = lax.optimization_barrier(jnp.mean(stream * stream, axis=1, keepdims=True))
    normed = (stream * lax.rsqrt(mean_sq + norm_eps) * norm_gain[None, :]).astype(jnp.bfloat16)
    gate = jnp.dot(normed, gate_up[:, 0, :], preferred_element_type=jnp.float32)
    upward = jnp.dot(normed, gate_up[:, 1, :], preferred_element_type=jnp.float32)
    hidden = (jax.nn.silu(gate) * upward).astype(jnp.bfloat16)
    layer_out = (stream + jnp.dot(hidden, w_down, preferred_element_type=jnp.float32)).astype(jnp.bfloat16)
    return (layer_out, state_next)
```

```python
import jax
import jax.numpy as jnp
from jax import lax
from jax.sharding import PartitionSpec as P

D = 5120
HD = 128
PH = 128


norm_eps = 1e-05


def visible(length, cache_len, steps_new):
    position = jnp.arange(cache_len + steps_new)[None, :]
    drafts = jnp.arange(steps_new)[:, None]
    return jnp.where(position < cache_len, position < length, position - cache_len <= drafts)


def attend_whole(request):
    queries, keys_new, values_new, keys_cache, values_cache, length = request
    steps_new = queries.shape[0]
    kv_heads = keys_new.shape[1] // HD
    groups = queries.shape[1] // keys_new.shape[1]
    q_heads = queries.reshape(steps_new, kv_heads, groups, HD)
    keys_all = jnp.concatenate([keys_cache, keys_new], 0).reshape(-1, kv_heads, HD)
    values_all = jnp.concatenate([values_cache, values_new], 0).reshape(-1, kv_heads, HD)
    scores = jnp.einsum(
        "qjgd,kjd->jgqk", q_heads, keys_all, preferred_element_type=jnp.float32
    ) * HD ** (-0.5)
    live = visible(length, keys_cache.shape[0], steps_new)
    scores = jnp.where(live[None, None], scores, -jnp.inf)
    peak = jnp.max(scores, axis=-1, keepdims=True)
    weights = jnp.exp(scores - peak)
    total = jnp.sum(weights, axis=-1)
    summed = jnp.einsum(
        "jgqk,kjd->qjgd",
        weights.astype(jnp.bfloat16),
        values_all,
        preferred_element_type=jnp.float32,
    )
    result = summed / jnp.transpose(total, (2, 0, 1))[..., None]
    return result.reshape(steps_new, -1).astype(jnp.bfloat16)


def ssm_scan(ssm_x, ssm_gate, ssm_b, ssm_c, ssm_dt, decay_rate, skip_gain, ssm_state, accepted):
    count = ssm_x.shape[0]
    steps_new = ssm_x.shape[1]
    heads = decay_rate.shape[0]
    inputs = ssm_x.astype(jnp.float32).reshape(count, steps_new, heads, PH)
    in_map = ssm_b.astype(jnp.float32)
    out_map = ssm_c.astype(jnp.float32)
    state = ssm_state
    kept = ssm_state
    outputs = []
    for t in range(steps_new):
        decay = jnp.exp(-ssm_dt[:, t, :] * decay_rate[None, :])
        driven = ssm_dt[:, t, :, None] * inputs[:, t]
        state = (
            decay[:, :, None, None] * state + driven[:, :, :, None] * in_map[:, t, None, None, :]
        )
        readout = jnp.einsum("rhpn,rn->rhp", state, out_map[:, t], precision=lax.Precision.HIGHEST)
        outputs.append(readout + skip_gain[None, :, None] * inputs[:, t])
        kept = jnp.where((accepted > t)[:, None, None, None], state, kept)
    stacked = jnp.stack(outputs, axis=1).reshape(count, steps_new, heads * PH)
    gated = stacked * jax.nn.silu(ssm_gate.astype(jnp.float32))
    return (gated.astype(jnp.bfloat16), kept)


def exchange(blocks, axis):
    return lax.all_to_all(blocks, axis, 0, 0, tiled=True)


def ring_gather(block, axis):
    size = lax.axis_size(axis)
    got = [block]
    for shift in range(1, size):
        got.append(lax.ppermute(block, axis, [(k, (k + shift) % size) for k in range(size)]))
    return jnp.stack(got)


def shards(
    resid,
    query,
    key_new,
    value_new,
    key_cache,
    value_cache,
    ctx_len,
    ssm_x,
    ssm_gate,
    ssm_b,
    ssm_c,
    ssm_dt,
    decay_rate,
    skip_gain,
    ssm_state,
    accepted,
    slot_of,
    w_out,
    norm_gain,
    gate_up,
    w_down,
):
    f32 = jnp.float32
    bf16 = jnp.bfloat16
    rows = lax.axis_size("row")
    cols = lax.axis_size("col")
    steps_new = query.shape[1]
    in_weights = lax.all_gather(jnp.transpose(gate_up, (1, 2, 0)), "grp", axis=0, tiled=False)
    down_weights = lax.all_gather(w_down, "grp", axis=0, tiled=True)

    requests = (query, key_new, value_new, key_cache, value_cache, ctx_len)
    attended = lax.map(attend_whole, requests)
    ssm_out, state_next = ssm_scan(
        ssm_x, ssm_gate, ssm_b, ssm_c, ssm_dt, decay_rate, skip_gain, ssm_state, accepted
    )
    mixed_local = jnp.concatenate([attended, ssm_out], axis=2).reshape(steps_new, -1)
    width = mixed_local.shape[1] // cols
    pieces = jnp.transpose(mixed_local.reshape(steps_new, cols, width), (1, 0, 2))
    mine = exchange(pieces, "col")
    by_slot = ring_gather(mine, "row").reshape(rows * cols, steps_new, width)
    behind = (lax.axis_index("row") - slot_of // cols) % rows
    mixed_req = jnp.take(by_slot, behind * cols + slot_of % cols, axis=0).reshape(-1, width)
    partial = jnp.dot(mixed_req, w_out, preferred_element_type=f32).astype(bf16)
    partial = partial.reshape(2, -1, partial.shape[1])
    half = jnp.sum(exchange(partial, "grp").astype(f32), axis=0).astype(bf16)
    half = exchange(half.reshape(cols, -1, half.shape[1]), "col")
    stream = resid.astype(f32) + jnp.sum(half.astype(f32), axis=0)
    scaled = (stream * norm_gain[None, :]).astype(bf16)
    spread = exchange(jnp.broadcast_to(scaled[None], (cols,) + scaled.shape), "col")
    tokens = spread.reshape(-1, spread.shape[2])
    squares = jnp.sum(jnp.square(tokens.astype(f32) / norm_gain[None, :]), axis=1, keepdims=True)
    high = squares.astype(bf16)
    low = (squares - high.astype(f32)).astype(bf16)
    units = in_weights.shape[2]
    sums = [
        lax.dot_general(
            tokens, in_weights[g, k], (((1,), (1,)), ((), ())), preferred_element_type=f32
        ).astype(bf16)
        for g in range(2)
        for k in range(2)
    ]
    packed = jnp.concatenate(sums + [high, low], axis=1)
    packed = packed.reshape(rows, -1, packed.shape[1])
    summed = jnp.sum(exchange(packed, "row").astype(f32), axis=0)
    mean_sq = (summed[:, 4 * units] + summed[:, 4 * units + 1]) / D
    summed = summed * lax.rsqrt(mean_sq[:, None] + norm_eps)
    hidden = jnp.concatenate(
        [
            jax.nn.silu(summed[:, 2 * g * units : (2 * g + 1) * units])
            * summed[:, (2 * g + 1) * units : (2 * g + 2) * units]
            for g in range(2)
        ],
        axis=1,
    ).astype(bf16)
    by_row = ring_gather(hidden, "row")
    order = (lax.axis_index("row") - jnp.arange(rows)) % rows
    hidden = jnp.take(by_row, order, axis=0).reshape(-1, hidden.shape[1])
    down = jnp.dot(hidden, down_weights, preferred_element_type=f32).astype(bf16)
    down = exchange(down.reshape(cols, -1, down.shape[1]), "col")
    layer_out = (stream + jnp.sum(down.astype(f32), axis=0)).astype(bf16)
    return (layer_out, state_next)


def solution(mesh):
    placed = (
        P(("grp", "col"), "row"),
        P(("row", "col"), None, "grp"),
        P(("row", "col"), None, "grp"),
        P(("row", "col"), None, "grp"),
        P(("row", "col"), None, "grp"),
        P(("row", "col"), None, "grp"),
        P(("row", "col")),
        P(("row", "col"), None, "grp"),
        P(("row", "col"), None, "grp"),
        P(("row", "col"), None, None),
        P(("row", "col"), None, None),
        P(("row", "col"), None, "grp"),
        P("grp"),
        P("grp"),
        P(("row", "col"), "grp", None, None),
        P(("row", "col")),
        P(),
        P(("grp", "col"), "row"),
        P("row"),
        P("row", None, ("grp", "col")),
        P(("grp", "col"), "row"),
    )
    return jax.shard_map(
        shards,
        mesh=mesh,
        in_specs=placed,
        out_specs=(P(("grp", "col"), "row"), P(("row", "col"), "grp", None, None)),
        check_vma=False,
    )
```

```python
import functools

import jax
import jax.numpy as jnp
from jax import lax
from jax.experimental import pallas as pl
from jax.experimental.pallas import tpu as pltpu
from jax.sharding import PartitionSpec as P

D = 5120
HD = 128
PH = 128


norm_eps = 1e-05


def fetch(pairs, sems):
    copies = [
        pltpu.make_async_copy(source, buffer, sems.at[i])
        for i, (source, buffer) in enumerate(pairs)
    ]
    for copy in copies:
        copy.start()
    return copies


def mixer_kernel(*refs):
    f32 = jnp.float32
    bf16 = jnp.bfloat16
    nt = (((1,), (1,)), ((), ()))
    small, (keys_hbm, values_hbm, state_hbm) = refs[:11], refs[11:14]
    pieces_ref = refs[14]
    buffers, (keys_ref, values_ref, state_ref, mixed_ref, sems, big_sems) = (
        refs[15:26],
        refs[26:],
    )
    copies = fetch(list(zip(small, buffers)), sems)
    kv_heads, _, head_size = keys_ref.shape
    heads = state_ref.shape[0] // kv_heads
    big = []
    for j in range(kv_heads):
        cols = pl.ds(j * head_size, head_size)
        big += [
            (state_hbm.at[0, pl.ds(j * heads, heads)], state_ref.at[pl.ds(j * heads, heads)]),
            (keys_hbm.at[0, :, cols], keys_ref.at[j]),
            (values_hbm.at[0, :, cols], values_ref.at[j]),
        ]
    big = fetch(big, big_sems)
    for copy in copies:
        copy.wait()
    (
        length_ref, query_ref, key_new_ref, value_new_ref, x_ref, gate_ref,
        in_map_ref, out_map_ref, dt_ref, rate_ref, skip_ref,
    ) = buffers
    drafts = query_ref.shape[1]
    groups = query_ref.shape[2] // (kv_heads * head_size)
    attended = query_ref.shape[2]

    dt = dt_ref[0]
    faded = [dt[0:1] * rate_ref[...]]
    for t in range(1, drafts):
        faded.append(faded[-1] + dt[t : t + 1] * rate_ref[...])
    fade = jnp.concatenate(faded, axis=0)
    row = lax.broadcasted_iota(jnp.int32, fade.shape, 0)
    kept = jnp.exp(-fade)
    out_map = out_map_ref[0]
    in_map = in_map_ref[0].astype(f32)
    readout = out_map.astype(f32)
    mixing = []
    for s in range(drafts):
        match = jnp.sum(readout * in_map[s : s + 1, :], axis=1, keepdims=True)
        since = jnp.where(row >= s, fade - faded[s], 0.0)
        share = jnp.where(row >= s, jnp.exp(-since) * match * dt[s : s + 1], 0.0)
        mixing.append(share + jnp.where(row == s, skip_ref[...], 0.0))
    out_maps = jnp.concatenate([out_map, out_map], axis=1)

    for j in range(kv_heads):
        for copy in big[3 * j : 3 * j + 3]:
            copy.wait()
        state = state_ref[j * heads : (j + 1) * heads].reshape(heads * PH, state_ref.shape[2])
        high = state.astype(bf16)
        low = (state - high.astype(f32)).astype(bf16)
        carried = lax.dot_general(
            out_maps, jnp.concatenate([high, low], axis=1), nt, preferred_element_type=f32
        )
        for i in range(heads):
            h = j * heads + i
            cols = slice(h * PH, (h + 1) * PH)
            inputs = x_ref[0, :, cols].astype(f32)
            gate = gate_ref[0, :, cols].astype(f32)
            y = kept[:, h : h + 1] * carried[:, i * PH : (i + 1) * PH]
            for s in range(drafts):
                y = y + mixing[s][:, h : h + 1] * inputs[s : s + 1]
            cols = slice(attended + h * PH, attended + (h + 1) * PH)
            mixed_ref[:, cols] = y * gate * jax.nn.sigmoid(gate)

        first = j * groups * head_size
        query = query_ref[0, :, first : first + groups * head_size].astype(f32)
        queries = jnp.concatenate(
            [query[:, g * head_size : (g + 1) * head_size] for g in range(groups)], axis=0
        )
        scores = lax.dot_general(
            queries.astype(bf16), keys_ref[j], nt, preferred_element_type=f32
        ) * head_size ** (-0.5)
        position = lax.broadcasted_iota(jnp.int32, scores.shape, 1)
        scores = jnp.where(position < length_ref[...], scores, -jnp.inf)
        peak = jnp.max(scores, axis=1, keepdims=True)
        draft = lax.broadcasted_iota(jnp.int32, peak.shape, 0) % drafts
        new_cols = slice(j * head_size, (j + 1) * head_size)
        keys_new = key_new_ref[0, :, new_cols].astype(f32)
        scores_new = []
        for u in range(drafts):
            score = jnp.sum(queries * keys_new[u : u + 1, :], axis=1, keepdims=True)
            score = jnp.where(draft >= u, score * head_size ** (-0.5), -jnp.inf)
            scores_new.append(score)
            peak = jnp.maximum(peak, score)
        weights = jnp.exp(scores - peak)
        total = jnp.sum(weights, axis=1, keepdims=True)
        summed = jnp.dot(weights.astype(bf16), values_ref[j], preferred_element_type=f32)
        values_new = value_new_ref[0, :, new_cols].astype(f32)
        for u in range(drafts):
            weight = jnp.exp(scores_new[u] - peak)
            total = total + weight
            summed = summed + weight.astype(bf16).astype(f32) * values_new[u : u + 1, :]
        result = summed / total
        for g in range(groups):
            cols = slice(first + g * head_size, first + (g + 1) * head_size)
            mixed_ref[:, cols] = result[g * drafts : (g + 1) * drafts]
    width = pieces_ref.shape[2]
    for c in range(pieces_ref.shape[0]):
        pieces_ref[c] = mixed_ref[:, c * width : (c + 1) * width].astype(bf16)


def mix(
    cols, query, key_new, value_new, key_cache, value_cache, ctx_len,
    ssm_x, ssm_gate, ssm_b, ssm_c, ssm_dt, decay_rate, skip_gain, ssm_state,
):
    kv_heads = key_new.shape[2] // HD
    features = query.shape[2] + ssm_x.shape[2]
    ctx_len = ctx_len.reshape(1, 1)
    small = (
        ctx_len, query, key_new, value_new, ssm_x, ssm_gate, ssm_b, ssm_c, ssm_dt,
        decay_rate.reshape(1, -1), skip_gain.reshape(1, -1),
    )
    big = (key_cache, value_cache, ssm_state)
    cached = (kv_heads, key_cache.shape[1], HD)
    return pl.pallas_call(
        mixer_kernel,
        in_specs=[pl.BlockSpec(memory_space=pltpu.HBM)] * (len(small) + len(big)),
        out_specs=pl.BlockSpec(memory_space=pltpu.VMEM),
        out_shape=jax.ShapeDtypeStruct((cols, query.shape[1], features // cols), jnp.bfloat16),
        scratch_shapes=[pltpu.VMEM(array.shape, array.dtype) for array in small]
        + [
            pltpu.VMEM(cached, key_cache.dtype),
            pltpu.VMEM(cached, value_cache.dtype),
            pltpu.VMEM(ssm_state.shape[1:], ssm_state.dtype),
            pltpu.VMEM((query.shape[1], features), jnp.float32),
            pltpu.SemaphoreType.DMA((len(small),)),
            pltpu.SemaphoreType.DMA((3 * kv_heads,)),
        ],
        compiler_params=pltpu.CompilerParams(vmem_limit_bytes=62 * 2**20),
        name="mixer",
    )(*small, *big)


def project_kernel(rows_ref, weights_ref, *out_refs):
    product = jnp.dot(rows_ref[...], weights_ref[...], preferred_element_type=jnp.float32)
    share = out_refs[0].shape[0]
    for i, out_ref in enumerate(out_refs):
        out_ref[...] = product[i * share : (i + 1) * share].astype(out_ref.dtype)


def merge_kernel(rows_ref, weights_ref, *refs):
    parts, out_ref = refs[:-1], refs[-1]
    product = jnp.dot(rows_ref[...], weights_ref[...], preferred_element_type=jnp.float32)
    share = parts[0].shape[0]
    for i, part in enumerate(parts):
        rows = slice(i * share, (i + 1) * share)
        out_ref[rows] = (product[rows] + part[...].astype(jnp.float32)).astype(out_ref.dtype)


def on_core(kernel, operands, out_shape, name, after=()):
    vmem = pl.BlockSpec(memory_space=pltpu.VMEM)
    count = len(operands)
    return pl.pallas_call(
        lambda *refs: kernel(*refs[:count], *refs[count + len(after) :]),
        in_specs=[vmem] * count + [pl.BlockSpec(memory_space=pl.ANY)] * len(after),
        out_specs=jax.tree.map(lambda _: vmem, out_shape),
        out_shape=out_shape,
        compiler_params=pltpu.CompilerParams(vmem_limit_bytes=16 * 2**20),
        name=name,
    )(*operands, *after)


def arrive_kernel(parts_ref, resid_ref, gain_ref, stream_ref, spread_ref):
    f32 = jnp.float32
    stream = resid_ref[...].astype(f32)
    for c in range(parts_ref.shape[0]):
        stream = stream + parts_ref[c].astype(f32)
    stream_ref[...] = stream
    scaled = (stream * gain_ref[...]).astype(spread_ref.dtype)
    for c in range(spread_ref.shape[0]):
        spread_ref[c] = scaled


def widen_kernel(rows, places, gain_ref, *refs):
    f32 = jnp.float32
    bf16 = jnp.bfloat16
    tokens, weights = refs[:rows], refs[rows : rows + len(places)]
    outs, ordered_ref = refs[rows + len(places) : -1], refs[-1]
    row = lax.axis_index("row")
    share = outs[0].shape[0]
    for q in range(rows):
        first = pl.multiple_of(lax.rem(q + rows - row, rows) * share, share)
        ordered_ref[pl.ds(first, share)] = tokens[q][...]
    for place, weight in zip(places, weights):
        units = weight.shape[0]
        sums = lax.dot_general(
            ordered_ref[...], weight[...], (((1,), (1,)), ((), ())), preferred_element_type=f32
        )
        if place + units == sum(w.shape[0] for w in weights):
            inverse = 1.0 / gain_ref[...]
            plain = ordered_ref[...].astype(f32) * inverse
            squares = jnp.sum(plain * plain, axis=1, keepdims=True)
            high = squares.astype(bf16).astype(f32)
            past = outs[0].shape[1] - (place + units)
            lane = lax.broadcasted_iota(jnp.int32, (squares.shape[0], past), 1)
            tail = jnp.where(lane == 0, high, jnp.where(lane == 1, squares - high, 0.0))
            sums = jnp.concatenate([sums, tail], axis=1)
        sums = sums.astype(bf16)
        for d in range(rows):
            outs[d][:, place : place + sums.shape[1]] = sums[d * share : (d + 1) * share]


def widen(tokens, gain, weights, places, rows):
    units = sum(weight.shape[0] for weight in weights)
    width = (units // 128 + 1) * 128
    share, depth = tokens[0].shape
    vmem = pl.BlockSpec(memory_space=pltpu.VMEM)
    return pl.pallas_call(
        functools.partial(widen_kernel, rows, places),
        in_specs=[vmem] * (1 + rows + len(weights)),
        out_specs=[vmem] * rows,
        out_shape=[jax.ShapeDtypeStruct((share, width), jnp.bfloat16)] * rows,
        scratch_shapes=[pltpu.VMEM((rows * share, depth), jnp.bfloat16)],
        compiler_params=pltpu.CompilerParams(vmem_limit_bytes=16 * 2**20),
        name="widen",
    )(gain, *tokens, *weights)


def narrow_kernel(rows, places, *refs):
    hidden_refs, weights = refs[:rows], refs[rows : rows + len(places)]
    outs, ordered_ref = refs[rows + len(places) : -1], refs[-1]
    row = lax.axis_index("row")
    share = hidden_refs[0].shape[0]
    for d in range(rows):
        first = pl.multiple_of(lax.rem(row + rows - d, rows) * share, share)
        ordered_ref[pl.ds(first, share)] = hidden_refs[d][...]
    down = None
    for place, weight in zip(places, weights):
        part = jnp.dot(
            ordered_ref[:, place : place + weight.shape[0]],
            weight[...],
            preferred_element_type=jnp.float32,
        )
        down = part if down is None else down + part
    down = down.astype(outs[0].dtype)
    for d in range(rows):
        outs[d][...] = down[d * share : (d + 1) * share]


def narrow(hidden, weights, places):
    rows = len(hidden)
    share, units = hidden[0].shape
    vmem = pl.BlockSpec(memory_space=pltpu.VMEM)
    return pl.pallas_call(
        functools.partial(narrow_kernel, rows, places),
        in_specs=[vmem] * (rows + len(weights)),
        out_specs=[vmem] * rows,
        out_shape=[jax.ShapeDtypeStruct((share, weights[0].shape[1]), jnp.bfloat16)] * rows,
        scratch_shapes=[pltpu.VMEM((rows * share, units), jnp.bfloat16)],
        compiler_params=pltpu.CompilerParams(vmem_limit_bytes=16 * 2**20),
        name="narrow",
    )(*hidden, *weights)


def state_kernel(accepted_ref, x_ref, in_map_ref, dt_ref, rate_ref, state_ref, *refs):
    f32 = jnp.float32
    out_ref = refs[-1]
    heads = state_ref.shape[1]
    dt = dt_ref[0]
    drafts = dt.shape[0]
    row = lax.broadcasted_iota(jnp.int32, dt.shape, 0)
    lane = lax.broadcasted_iota(jnp.int32, dt.shape, 1)
    taken = row < accepted_ref[0]
    step = jnp.where(taken, dt, 0.0) * rate_ref[...]
    after = [jnp.zeros_like(step[:1])]
    for t in range(drafts - 1, 0, -1):
        after.insert(0, after[0] + step[t : t + 1])
    whole = jnp.exp(-(after[0] + step[:1]))
    share = jnp.where(taken, jnp.exp(-jnp.concatenate(after, axis=0)) * dt, 0.0)
    terms = []
    for i in range(heads):
        mine = lane == pl.program_id(0) * heads + i
        part = jnp.sum(jnp.where(mine, share, 0.0), axis=1, keepdims=True)
        terms.append(part * x_ref[0, :, i * PH : (i + 1) * PH].astype(f32))
    added = lax.dot_general(
        jnp.concatenate(terms, axis=1),
        in_map_ref[0].astype(f32),
        (((0,), (0,)), ((), ())),
        precision=lax.Precision.HIGHEST,
        preferred_element_type=f32,
    )
    for i in range(heads):
        mine = lane[:1] == pl.program_id(0) * heads + i
        keep = jnp.sum(jnp.where(mine, whole, 0.0), axis=1, keepdims=True)
        out_ref[0, i] = keep * state_ref[0, i] + added[i * PH : (i + 1) * PH]


def final_state(ssm_x, ssm_b, ssm_dt, decay_rate, ssm_state, accepted, after):
    steps = 4
    heads = ssm_state.shape[1] // steps

    def whole(array):
        return pl.BlockSpec(array.shape, lambda j: (0,) * array.ndim)

    decay_rate = decay_rate.reshape(1, -1)
    block = pl.BlockSpec((1, heads) + ssm_state.shape[2:], lambda j: (0, j, 0, 0))
    return pl.pallas_call(
        state_kernel,
        grid=(steps,),
        in_specs=[
            pl.BlockSpec(memory_space=pltpu.SMEM),
            pl.BlockSpec(ssm_x.shape[:2] + (heads * PH,), lambda j: (0, 0, j)),
            whole(ssm_b),
            whole(ssm_dt),
            whole(decay_rate),
            block,
            pl.BlockSpec(memory_space=pl.ANY),
        ],
        out_specs=block,
        out_shape=jax.ShapeDtypeStruct(ssm_state.shape, ssm_state.dtype),
        compiler_params=pltpu.CompilerParams(vmem_limit_bytes=16 * 2**20),
        name="final_state",
    )(accepted, ssm_x, ssm_b, ssm_dt, decay_rate, ssm_state, after)


def exchange(blocks, axis, groups=None):
    return lax.all_to_all(blocks, axis, 0, 0, tiled=True, axis_index_groups=groups)


def shifted(blocks, axis):
    size = lax.axis_size(axis)
    return [blocks[0]] + [
        lax.ppermute(blocks[shift], axis, [(k, (k + shift) % size) for k in range(size)])
        for shift in range(1, size)
    ]


def around(blocks, size, sign):
    outer = lax.axis_size("col") // size
    return [blocks[0]] + [
        lax.ppermute(
            blocks[shift],
            "col",
            [
                (o * size + i, o * size + (i + sign * shift) % size)
                for o in range(outer)
                for i in range(size)
            ],
        )
        for shift in range(1, size)
    ]


def from_partner(weights, cut):
    swap = [(0, 1), (1, 0)]
    return [
        lax.ppermute(weights[first : first + cut], "grp", swap)
        for first in range(0, weights.shape[0], cut)
    ]


def shards(
    resid,
    query,
    key_new,
    value_new,
    key_cache,
    value_cache,
    ctx_len,
    ssm_x,
    ssm_gate,
    ssm_b,
    ssm_c,
    ssm_dt,
    decay_rate,
    skip_gain,
    ssm_state,
    accepted,
    slot_of,
    w_out,
    norm_gain,
    gate_up,
    w_down,
):
    f32 = jnp.float32
    bf16 = jnp.bfloat16
    rows = lax.axis_size("row")
    cols = lax.axis_size("col")
    steps_new = query.shape[1]
    inner = 4
    lines = [[o * inner + i for o in range(cols // inner)] for i in range(inner)]
    pieces = mix(
        cols, query, key_new, value_new, key_cache, value_cache, ctx_len,
        ssm_x, ssm_gate, ssm_b, ssm_c, ssm_dt, decay_rate, skip_gain, ssm_state,
    )
    width = pieces.shape[2]
    mine = exchange(pieces, "col")
    by_slot = jnp.concatenate(shifted([mine] * rows, "row"), axis=0)
    behind = (lax.axis_index("row") - slot_of // cols) % rows
    place = (behind * cols + slot_of % cols).reshape(2, -1)
    other = lax.axis_index("grp") ^ 1
    place = jnp.where(other == 0, place, place[::-1]).reshape(-1)
    mixed_req = jnp.take(by_slot, place, axis=0).reshape(2, -1, width)
    swap = [(0, 1), (1, 0)]
    sent = jax.ShapeDtypeStruct((mixed_req.shape[1] // 2, w_out.shape[1]), bf16)
    for_other = on_core(project_kernel, (mixed_req[0], w_out), [sent] * 2, "project")
    from_other = [lax.ppermute(part, "grp", swap) for part in for_other]
    held = jax.ShapeDtypeStruct((mixed_req.shape[1], w_out.shape[1]), bf16)
    half = on_core(merge_kernel, (mixed_req[1], w_out, *from_other), held, "merge")
    half, gate_up, w_down, gain = lax.optimization_barrier((half, gate_up, w_down, norm_gain))
    state_next = final_state(ssm_x, ssm_b, ssm_dt, decay_rate, ssm_state, accepted, half)
    half = exchange(half.reshape(cols, -1, half.shape[1]), "col")
    units = gate_up.shape[2]
    in_weights = jnp.transpose(gate_up, (1, 2, 0)).reshape(2 * units, -1)
    in_pieces = from_partner(in_weights, 128)
    whole = 2 * units // 128
    in_places = [128 * i for i in range(whole)] + [128 * whole + 2 * units, 128 * whole]
    if 2 * units % 128 == 0:
        in_places = in_places[:-2] + in_places[-1:]
    in_pieces = in_pieces + [in_weights]
    down_pieces = from_partner(w_down, 128) + [w_down]
    padded = -(-units // 128) * 128
    down_places = list(range(0, units, 128)) + [padded]
    gain = gain.reshape(1, -1)
    stream, spread = on_core(
        arrive_kernel,
        (half, resid, gain),
        [
            jax.ShapeDtypeStruct(resid.shape, f32),
            jax.ShapeDtypeStruct((cols // inner,) + resid.shape, bf16),
        ],
        "arrive",
    )
    spread = exchange(spread, "col", lines)
    tokens = [
        block.reshape(-1, block.shape[2]) for block in around([spread] * inner, inner, 1)
    ]
    sums = shifted(widen(tokens, gain, in_pieces, in_places, rows), "row")
    summed = functools.reduce(jnp.add, [part.astype(f32) for part in sums])
    mean_sq = (summed[:, 4 * units] + summed[:, 4 * units + 1]) / D
    summed = summed * lax.rsqrt(mean_sq[:, None] + norm_eps)
    first = 128 * whole
    gate = [summed[:, :units], summed[:, first : first + units]]
    up = [
        jnp.concatenate(
            [summed[:, units:first], summed[:, first + 2 * units : 4 * units]], axis=1
        ),
        summed[:, first + units : first + 2 * units],
    ]
    hidden = [(jax.nn.silu(g) * u).astype(bf16) for g, u in zip(gate, up)]
    blank = jnp.zeros((hidden[0].shape[0], padded - units), bf16)
    hidden = jnp.concatenate([hidden[0], blank, hidden[1]], axis=1)
    down = narrow(shifted([hidden] * rows, "row"), down_pieces, down_places)
    down = around(down, inner, -1)
    down = functools.reduce(jnp.add, [part.astype(f32) for part in down]).astype(bf16)
    down = exchange(down.reshape(cols // inner, -1, down.shape[1]), "col", lines)
    layer_out = (stream + jnp.sum(down.astype(f32), axis=0)).astype(bf16)
    return (layer_out, state_next)


def solution(mesh):
    placed = (
        P(("grp", "col"), "row"),
        P(("row", "col"), None, "grp"),
        P(("row", "col"), None, "grp"),
        P(("row", "col"), None, "grp"),
        P(("row", "col"), None, "grp"),
        P(("row", "col"), None, "grp"),
        P(("row", "col")),
        P(("row", "col"), None, "grp"),
        P(("row", "col"), None, "grp"),
        P(("row", "col"), None, None),
        P(("row", "col"), None, None),
        P(("row", "col"), None, "grp"),
        P("grp"),
        P("grp"),
        P(("row", "col"), "grp", None, None),
        P(("row", "col")),
        P(),
        P(("grp", "col"), "row"),
        P("row"),
        P("row", None, ("grp", "col")),
        P(("grp", "col"), "row"),
    )
    return jax.shard_map(
        shards,
        mesh=mesh,
        in_specs=placed,
        out_specs=(P(("grp", "col"), "row"), P(("row", "col"), "grp", None, None)),
        check_vma=False,
    )
```

```python
import functools

import jax
import jax.numpy as jnp
from jax import lax
from jax.experimental import pallas as pl
from jax.experimental.pallas import tpu as pltpu
from jax.sharding import PartitionSpec as P

D = 5120
HD = 128
PH = 128


norm_eps = 1e-05


def fetch(pairs, sems):
    copies = [
        pltpu.make_async_copy(source, buffer, sems.at[i])
        for i, (source, buffer) in enumerate(pairs)
    ]
    for copy in copies:
        copy.start()
    return copies


def mixer_kernel(*refs):
    f32 = jnp.float32
    bf16 = jnp.bfloat16
    nt = (((1,), (1,)), ((), ()))
    small, (keys_hbm, values_hbm, state_hbm) = refs[:11], refs[11:14]
    pieces_ref = refs[14]
    buffers, (keys_ref, values_ref, state_ref, mixed_ref, sems, big_sems) = (
        refs[15:26],
        refs[26:],
    )
    copies = fetch(list(zip(small, buffers)), sems)
    state_copy, key_copy, value_copy = [
        pltpu.make_async_copy(source.at[0], buffer, big_sems.at[i])
        for i, (source, buffer) in enumerate(
            [(state_hbm, state_ref), (keys_hbm, keys_ref), (values_hbm, values_ref)]
        )
    ]
    state_copy.start()
    key_copy.start()
    for copy in copies:
        copy.wait()
    (
        length_ref, query_ref, key_new_ref, value_new_ref, x_ref, gate_ref,
        in_map_ref, out_map_ref, dt_ref, rate_ref, skip_ref,
    ) = buffers
    drafts = query_ref.shape[1]
    head_size = HD
    kv_heads = keys_ref.shape[1] // head_size
    heads = state_ref.shape[0] // kv_heads
    groups = query_ref.shape[2] // (kv_heads * head_size)
    attended = query_ref.shape[2]

    dt = dt_ref[0]
    faded = [dt[0:1] * rate_ref[...]]
    for t in range(1, drafts):
        faded.append(faded[-1] + dt[t : t + 1] * rate_ref[...])
    fade = jnp.concatenate(faded, axis=0)
    row = lax.broadcasted_iota(jnp.int32, fade.shape, 0)
    kept = jnp.exp(-fade)
    out_map = out_map_ref[0]
    in_map = in_map_ref[0].astype(f32)
    readout = out_map.astype(f32)
    mixing = []
    for s in range(drafts):
        match = jnp.sum(readout * in_map[s : s + 1, :], axis=1, keepdims=True)
        since = jnp.where(row >= s, fade - faded[s], 0.0)
        share = jnp.where(row >= s, jnp.exp(-since) * match * dt[s : s + 1], 0.0)
        mixing.append(share + jnp.where(row == s, skip_ref[...], 0.0))
    out_maps = jnp.concatenate([out_map, out_map], axis=1)

    state_copy.wait()
    value_copy.start()
    for j in range(kv_heads):
        state = state_ref[j * heads : (j + 1) * heads].reshape(heads * PH, state_ref.shape[2])
        high = state.astype(bf16)
        low = (state - high.astype(f32)).astype(bf16)
        carried = lax.dot_general(
            out_maps, jnp.concatenate([high, low], axis=1), nt, preferred_element_type=f32
        )
        for i in range(heads):
            h = j * heads + i
            cols = slice(h * PH, (h + 1) * PH)
            inputs = x_ref[0, :, cols].astype(f32)
            gate = gate_ref[0, :, cols].astype(f32)
            y = kept[:, h : h + 1] * carried[:, i * PH : (i + 1) * PH]
            for s in range(drafts):
                y = y + mixing[s][:, h : h + 1] * inputs[s : s + 1]
            cols = slice(attended + h * PH, attended + (h + 1) * PH)
            mixed_ref[:, cols] = y * gate * jax.nn.sigmoid(gate)

    key_copy.wait()
    held = []
    for j in range(kv_heads):
        first = j * groups * head_size
        query = query_ref[0, :, first : first + groups * head_size].astype(f32)
        queries = jnp.concatenate(
            [query[:, g * head_size : (g + 1) * head_size] for g in range(groups)], axis=0
        )
        scores = lax.dot_general(
            queries.astype(bf16), keys_ref[:, j * head_size : (j + 1) * head_size], nt, preferred_element_type=f32
        ) * head_size ** (-0.5)
        position = lax.broadcasted_iota(jnp.int32, scores.shape, 1)
        scores = jnp.where(position < length_ref[...], scores, -jnp.inf)
        peak = jnp.max(scores, axis=1, keepdims=True)
        draft = lax.broadcasted_iota(jnp.int32, peak.shape, 0) % drafts
        new_cols = slice(j * head_size, (j + 1) * head_size)
        keys_new = key_new_ref[0, :, new_cols].astype(f32)
        scores_new = []
        for u in range(drafts):
            score = jnp.sum(queries * keys_new[u : u + 1, :], axis=1, keepdims=True)
            score = jnp.where(draft >= u, score * head_size ** (-0.5), -jnp.inf)
            scores_new.append(score)
            peak = jnp.maximum(peak, score)
        weights = jnp.exp(scores - peak)
        total = jnp.sum(weights, axis=1, keepdims=True)
        held.append((weights.astype(bf16), total, [jnp.exp(s - peak) for s in scores_new]))

    value_copy.wait()
    for j in range(kv_heads):
        first = j * groups * head_size
        new_cols = slice(j * head_size, (j + 1) * head_size)
        weights, total, weights_new = held[j]
        summed = jnp.dot(weights, values_ref[:, new_cols], preferred_element_type=f32)
        values_new = value_new_ref[0, :, new_cols].astype(f32)
        for u in range(drafts):
            weight = weights_new[u]
            total = total + weight
            summed = summed + weight.astype(bf16).astype(f32) * values_new[u : u + 1, :]
        result = summed / total
        for g in range(groups):
            cols = slice(first + g * head_size, first + (g + 1) * head_size)
            mixed_ref[:, cols] = result[g * drafts : (g + 1) * drafts]
    width = pieces_ref.shape[3]
    cols = pieces_ref.shape[1]
    for c in range(cols):
        piece = mixed_ref[:, c * width : (c + 1) * width].astype(bf16)
        for r in range(pieces_ref.shape[0]):
            pieces_ref[r, c] = piece


def mix(
    rows, cols, query, key_new, value_new, key_cache, value_cache, ctx_len,
    ssm_x, ssm_gate, ssm_b, ssm_c, ssm_dt, decay_rate, skip_gain, ssm_state,
):
    kv_heads = key_new.shape[2] // HD
    features = query.shape[2] + ssm_x.shape[2]
    ctx_len = ctx_len.reshape(1, 1)
    small = (
        ctx_len, query, key_new, value_new, ssm_x, ssm_gate, ssm_b, ssm_c, ssm_dt,
        decay_rate.reshape(1, -1), skip_gain.reshape(1, -1),
    )
    big = (key_cache, value_cache, ssm_state)
    cached = key_cache.shape[1:]
    return pl.pallas_call(
        mixer_kernel,
        in_specs=[pl.BlockSpec(memory_space=pltpu.HBM)] * (len(small) + len(big)),
        out_specs=pl.BlockSpec(memory_space=pltpu.VMEM),
        out_shape=jax.ShapeDtypeStruct(
            (rows, cols, query.shape[1], features // cols), jnp.bfloat16
        ),
        scratch_shapes=[pltpu.VMEM(array.shape, array.dtype) for array in small]
        + [
            pltpu.VMEM(cached, key_cache.dtype),
            pltpu.VMEM(cached, value_cache.dtype),
            pltpu.VMEM(ssm_state.shape[1:], ssm_state.dtype),
            pltpu.VMEM((query.shape[1], features), jnp.float32),
            pltpu.SemaphoreType.DMA((len(small),)),
            pltpu.SemaphoreType.DMA((3,)),
        ],
        compiler_params=pltpu.CompilerParams(vmem_limit_bytes=62 * 2**20),
        name="mixer",
    )(*small, *big)


def project_kernel(rows_ref, weights_ref, out_ref):
    out_ref[...] = jnp.dot(
        rows_ref[...], weights_ref[...], preferred_element_type=jnp.float32
    ).astype(out_ref.dtype)


def merge_kernel(rows_ref, weights_ref, part_ref, out_ref):
    product = jnp.dot(rows_ref[...], weights_ref[...], preferred_element_type=jnp.float32)
    out_ref[...] = (product + part_ref[...].astype(jnp.float32)).astype(out_ref.dtype)


def on_core(kernel, operands, out_shape, name, after=()):
    vmem = pl.BlockSpec(memory_space=pltpu.VMEM)
    count = len(operands)
    return pl.pallas_call(
        lambda *refs: kernel(*refs[:count], *refs[count + len(after) :]),
        in_specs=[vmem] * count + [pl.BlockSpec(memory_space=pl.ANY)] * len(after),
        out_specs=jax.tree.map(lambda _: vmem, out_shape),
        out_shape=out_shape,
        compiler_params=pltpu.CompilerParams(vmem_limit_bytes=16 * 2**20),
        name=name,
    )(*operands, *after)


def arrive_kernel(parts_ref, resid_ref, gain_ref, stream_ref, spread_ref):
    f32 = jnp.float32
    stream = resid_ref[...].astype(f32)
    for c in range(parts_ref.shape[0]):
        stream = stream + parts_ref[c].astype(f32)
    stream_ref[...] = stream
    scaled = (stream * gain_ref[...]).astype(spread_ref.dtype)
    for c in range(spread_ref.shape[0]):
        spread_ref[c] = scaled


def widen_kernel(rows, places, gain_ref, *refs):
    f32 = jnp.float32
    bf16 = jnp.bfloat16
    tokens, weights = refs[:rows], refs[rows : rows + len(places)]
    outs, ordered_ref = refs[rows + len(places) : -1], refs[-1]
    row = lax.axis_index("row")
    share = outs[0].shape[0]
    for q in range(rows):
        first = pl.multiple_of(lax.rem(q + rows - row, rows) * share, share)
        ordered_ref[pl.ds(first, share)] = tokens[q][...]
    for place, weight in zip(places, weights):
        units = weight.shape[0]
        sums = lax.dot_general(
            ordered_ref[...], weight[...], (((1,), (1,)), ((), ())), preferred_element_type=f32
        )
        if place + units == sum(w.shape[0] for w in weights):
            inverse = 1.0 / gain_ref[...]
            plain = ordered_ref[...].astype(f32) * inverse
            squares = jnp.sum(plain * plain, axis=1, keepdims=True)
            high = squares.astype(bf16).astype(f32)
            past = outs[0].shape[1] - (place + units)
            lane = lax.broadcasted_iota(jnp.int32, (squares.shape[0], past), 1)
            tail = jnp.where(lane == 0, high, jnp.where(lane == 1, squares - high, 0.0))
            sums = jnp.concatenate([sums, tail], axis=1)
        sums = sums.astype(bf16)
        for d in range(rows):
            outs[d][:, place : place + sums.shape[1]] = sums[d * share : (d + 1) * share]


def widen(tokens, gain, weights, places, rows):
    units = sum(weight.shape[0] for weight in weights)
    width = (units // 128 + 1) * 128
    share, depth = tokens[0].shape
    vmem = pl.BlockSpec(memory_space=pltpu.VMEM)
    return pl.pallas_call(
        functools.partial(widen_kernel, rows, places),
        in_specs=[vmem] * (1 + rows + len(weights)),
        out_specs=[vmem] * rows,
        out_shape=[jax.ShapeDtypeStruct((share, width), jnp.bfloat16)] * rows,
        scratch_shapes=[pltpu.VMEM((rows * share, depth), jnp.bfloat16)],
        compiler_params=pltpu.CompilerParams(vmem_limit_bytes=16 * 2**20),
        name="widen",
    )(gain, *tokens, *weights)


def narrow_kernel(rows, places, *refs):
    hidden_refs, weights = refs[:rows], refs[rows : rows + len(places)]
    outs, ordered_ref = refs[rows + len(places) : -1], refs[-1]
    row = lax.axis_index("row")
    share = hidden_refs[0].shape[0]
    for d in range(rows):
        first = pl.multiple_of(lax.rem(row + rows - d, rows) * share, share)
        ordered_ref[pl.ds(first, share)] = hidden_refs[d][...]
    down = None
    for place, weight in zip(places, weights):
        part = jnp.dot(
            ordered_ref[:, place : place + weight.shape[0]],
            weight[...],
            preferred_element_type=jnp.float32,
        )
        down = part if down is None else down + part
    down = down.astype(outs[0].dtype)
    for d in range(rows):
        outs[d][...] = down[d * share : (d + 1) * share]


def narrow(hidden, weights, places):
    rows = len(hidden)
    share, units = hidden[0].shape
    vmem = pl.BlockSpec(memory_space=pltpu.VMEM)
    return pl.pallas_call(
        functools.partial(narrow_kernel, rows, places),
        in_specs=[vmem] * (rows + len(weights)),
        out_specs=[vmem] * rows,
        out_shape=[jax.ShapeDtypeStruct((share, weights[0].shape[1]), jnp.bfloat16)] * rows,
        scratch_shapes=[pltpu.VMEM((rows * share, units), jnp.bfloat16)],
        compiler_params=pltpu.CompilerParams(vmem_limit_bytes=16 * 2**20),
        name="narrow",
    )(*hidden, *weights)


def state_kernel(accepted_ref, x_ref, in_map_ref, dt_ref, rate_ref, state_ref, *refs):
    f32 = jnp.float32
    out_ref = refs[-1]
    heads = state_ref.shape[1]
    dt = dt_ref[0]
    drafts = dt.shape[0]
    row = lax.broadcasted_iota(jnp.int32, dt.shape, 0)
    lane = lax.broadcasted_iota(jnp.int32, dt.shape, 1)
    taken = row < accepted_ref[0]
    step = jnp.where(taken, dt, 0.0) * rate_ref[...]
    after = [jnp.zeros_like(step[:1])]
    for t in range(drafts - 1, 0, -1):
        after.insert(0, after[0] + step[t : t + 1])
    whole = jnp.exp(-(after[0] + step[:1]))
    share = jnp.where(taken, jnp.exp(-jnp.concatenate(after, axis=0)) * dt, 0.0)
    terms = []
    for i in range(heads):
        mine = lane == pl.program_id(0) * heads + i
        part = jnp.sum(jnp.where(mine, share, 0.0), axis=1, keepdims=True)
        terms.append(part * x_ref[0, :, i * PH : (i + 1) * PH].astype(f32))
    added = lax.dot_general(
        jnp.concatenate(terms, axis=1),
        in_map_ref[0].astype(f32),
        (((0,), (0,)), ((), ())),
        precision=lax.Precision.HIGHEST,
        preferred_element_type=f32,
    )
    for i in range(heads):
        mine = lane[:1] == pl.program_id(0) * heads + i
        keep = jnp.sum(jnp.where(mine, whole, 0.0), axis=1, keepdims=True)
        out_ref[0, i] = keep * state_ref[0, i] + added[i * PH : (i + 1) * PH]


def final_state(ssm_x, ssm_b, ssm_dt, decay_rate, ssm_state, accepted, after):
    steps = 4
    heads = ssm_state.shape[1] // steps

    def whole(array):
        return pl.BlockSpec(array.shape, lambda j: (0,) * array.ndim)

    decay_rate = decay_rate.reshape(1, -1)
    block = pl.BlockSpec((1, heads) + ssm_state.shape[2:], lambda j: (0, j, 0, 0))
    return pl.pallas_call(
        state_kernel,
        grid=(steps,),
        in_specs=[
            pl.BlockSpec(memory_space=pltpu.SMEM),
            pl.BlockSpec(ssm_x.shape[:2] + (heads * PH,), lambda j: (0, 0, j)),
            whole(ssm_b),
            whole(ssm_dt),
            whole(decay_rate),
            block,
            pl.BlockSpec(memory_space=pl.ANY),
        ],
        out_specs=block,
        out_shape=jax.ShapeDtypeStruct(ssm_state.shape, ssm_state.dtype),
        compiler_params=pltpu.CompilerParams(vmem_limit_bytes=16 * 2**20),
        name="final_state",
    )(accepted, ssm_x, ssm_b, ssm_dt, decay_rate, ssm_state, after)


def exchange(blocks, axis, groups=None):
    return lax.all_to_all(blocks, axis, 0, 0, tiled=True, axis_index_groups=groups)


def shifted(blocks, axis):
    size = lax.axis_size(axis)
    return [blocks[0]] + [
        lax.ppermute(blocks[shift], axis, [(k, (k + shift) % size) for k in range(size)])
        for shift in range(1, size)
    ]


def around(blocks, size, sign):
    outer = lax.axis_size("col") // size
    return [blocks[0]] + [
        lax.ppermute(
            blocks[shift],
            "col",
            [
                (o * size + i, o * size + (i + sign * shift) % size)
                for o in range(outer)
                for i in range(size)
            ],
        )
        for shift in range(1, size)
    ]


def from_partner(weights):
    return lax.ppermute(weights, "grp", [(0, 1), (1, 0)])


def shards(
    resid,
    query,
    key_new,
    value_new,
    key_cache,
    value_cache,
    ctx_len,
    ssm_x,
    ssm_gate,
    ssm_b,
    ssm_c,
    ssm_dt,
    decay_rate,
    skip_gain,
    ssm_state,
    accepted,
    slot_of,
    w_out,
    norm_gain,
    gate_up,
    w_down,
):
    f32 = jnp.float32
    bf16 = jnp.bfloat16
    rows = lax.axis_size("row")
    cols = lax.axis_size("col")
    steps_new = query.shape[1]
    inner = 4
    lines = [[o * inner + i for o in range(cols // inner)] for i in range(inner)]
    pieces = mix(
        rows, cols, query, key_new, value_new, key_cache, value_cache, ctx_len,
        ssm_x, ssm_gate, ssm_b, ssm_c, ssm_dt, decay_rate, skip_gain, ssm_state,
    )
    width = pieces.shape[3]
    by_slot = exchange(pieces.reshape((rows * cols,) + pieces.shape[2:]), ("row", "col"))
    place = slot_of.reshape(2, -1)
    place = jnp.where(lax.axis_index("grp") == 1, place, place[::-1])
    for_other = jnp.take(by_slot, place[0], axis=0).reshape(-1, width)
    own = jnp.take(by_slot, place[1], axis=0).reshape(-1, width)
    held = jax.ShapeDtypeStruct((own.shape[0], w_out.shape[1]), bf16)
    for_other = on_core(project_kernel, (for_other, w_out), held, "project")
    half = on_core(merge_kernel, (own, w_out, from_partner(for_other)), held, "merge")
    half, gate_up, w_down, gain = lax.optimization_barrier((half, gate_up, w_down, norm_gain))
    state_next = final_state(ssm_x, ssm_b, ssm_dt, decay_rate, ssm_state, accepted, half)
    half = exchange(half.reshape(cols, -1, half.shape[1]), "col")
    units = gate_up.shape[2]
    in_weights = jnp.transpose(gate_up, (1, 2, 0)).reshape(2 * units, -1)
    in_pieces = [from_partner(in_weights), in_weights]
    in_places = [0, 2 * units]
    down_pieces = [from_partner(w_down), w_down]
    padded = -(-units // 128) * 128
    down_places = [0, padded]
    gain = gain.reshape(1, -1)
    stream, spread = on_core(
        arrive_kernel,
        (half, resid, gain),
        [
            jax.ShapeDtypeStruct(resid.shape, f32),
            jax.ShapeDtypeStruct((cols // inner,) + resid.shape, bf16),
        ],
        "arrive",
        [piece[:16, :128] for piece in in_pieces[:-1] + down_pieces[:-1]],
    )
    spread = exchange(spread, "col", lines)
    tokens = [
        block.reshape(-1, block.shape[2]) for block in around([spread] * inner, inner, 1)
    ]
    sums = shifted(widen(tokens, gain, in_pieces, in_places, rows), "row")
    summed = functools.reduce(jnp.add, [part.astype(f32) for part in sums])
    mean_sq = (summed[:, 4 * units] + summed[:, 4 * units + 1]) / D
    summed = summed * lax.rsqrt(mean_sq[:, None] + norm_eps)
    gate = [summed[:, :units], summed[:, 2 * units : 3 * units]]
    up = [summed[:, units : 2 * units], summed[:, 3 * units : 4 * units]]
    hidden = [(jax.nn.silu(g) * u).astype(bf16) for g, u in zip(gate, up)]
    blank = jnp.zeros((hidden[0].shape[0], padded - units), bf16)
    hidden = jnp.concatenate([hidden[0], blank, hidden[1]], axis=1)
    down = narrow(shifted([hidden] * rows, "row"), down_pieces, down_places)
    down = around(down, inner, -1)
    down = functools.reduce(jnp.add, [part.astype(f32) for part in down]).astype(bf16)
    down = exchange(down.reshape(cols // inner, -1, down.shape[1]), "col", lines)
    layer_out = (stream + jnp.sum(down.astype(f32), axis=0)).astype(bf16)
    return (layer_out, state_next)


def solution(mesh):
    placed = (
        P(("grp", "col"), "row"),
        P(("row", "col"), None, "grp"),
        P(("row", "col"), None, "grp"),
        P(("row", "col"), None, "grp"),
        P(("row", "col"), None, "grp"),
        P(("row", "col"), None, "grp"),
        P(("row", "col")),
        P(("row", "col"), None, "grp"),
        P(("row", "col"), None, "grp"),
        P(("row", "col"), None, None),
        P(("row", "col"), None, None),
        P(("row", "col"), None, "grp"),
        P("grp"),
        P("grp"),
        P(("row", "col"), "grp", None, None),
        P(("row", "col")),
        P(),
        P(("grp", "col"), "row"),
        P("row"),
        P("row", None, ("grp", "col")),
        P(("grp", "col"), "row"),
    )
    return jax.shard_map(
        shards,
        mesh=mesh,
        in_specs=placed,
        out_specs=(P(("grp", "col"), "row"), P(("row", "col"), "grp", None, None)),
        check_vma=False,
    )
```

```python
import functools

import jax
import jax.numpy as jnp
from jax import lax
from jax.experimental import pallas as pl
from jax.experimental.pallas import tpu as pltpu
from jax.sharding import PartitionSpec as P

D = 5120
HD = 128
PH = 128


norm_eps = 1e-05


def fetch(pairs, sems):
    copies = [
        pltpu.make_async_copy(source, buffer, sems.at[i])
        for i, (source, buffer) in enumerate(pairs)
    ]
    for copy in copies:
        copy.start()
    return copies


def mixer_kernel(*refs):
    f32 = jnp.float32
    bf16 = jnp.bfloat16
    nt = (((1,), (1,)), ((), ()))
    small, (keys_hbm, values_hbm, state_hbm) = refs[:11], refs[11:14]
    pieces_ref = refs[14]
    buffers, (keys_ref, values_ref, state_ref, mixed_ref, sems, big_sems) = (
        refs[15:26],
        refs[26:],
    )
    copies = fetch(list(zip(small, buffers)), sems)
    state_copy, key_copy, value_copy = [
        pltpu.make_async_copy(source.at[0], buffer, big_sems.at[i])
        for i, (source, buffer) in enumerate(
            [(state_hbm, state_ref), (keys_hbm, keys_ref), (values_hbm, values_ref)]
        )
    ]
    state_copy.start()
    key_copy.start()
    for copy in copies:
        copy.wait()
    (
        length_ref, query_ref, key_new_ref, value_new_ref, x_ref, gate_ref,
        in_map_ref, out_map_ref, dt_ref, rate_ref, skip_ref,
    ) = buffers
    drafts = query_ref.shape[1]
    head_size = HD
    kv_heads = keys_ref.shape[1] // head_size
    heads = state_ref.shape[0] // kv_heads
    groups = query_ref.shape[2] // (kv_heads * head_size)
    attended = query_ref.shape[2]

    dt = dt_ref[0]
    faded = [dt[0:1] * rate_ref[...]]
    for t in range(1, drafts):
        faded.append(faded[-1] + dt[t : t + 1] * rate_ref[...])
    fade = jnp.concatenate(faded, axis=0)
    row = lax.broadcasted_iota(jnp.int32, fade.shape, 0)
    kept = jnp.exp(-fade)
    out_map = out_map_ref[0]
    in_map = in_map_ref[0].astype(f32)
    readout = out_map.astype(f32)
    mixing = []
    for s in range(drafts):
        match = jnp.sum(readout * in_map[s : s + 1, :], axis=1, keepdims=True)
        since = jnp.where(row >= s, fade - faded[s], 0.0)
        share = jnp.where(row >= s, jnp.exp(-since) * match * dt[s : s + 1], 0.0)
        mixing.append(share + jnp.where(row == s, skip_ref[...], 0.0))
    out_maps = jnp.concatenate([out_map, out_map], axis=1)

    state_copy.wait()
    value_copy.start()
    for j in range(kv_heads):
        state = state_ref[j * heads : (j + 1) * heads].reshape(heads * PH, state_ref.shape[2])
        high = state.astype(bf16)
        low = (state - high.astype(f32)).astype(bf16)
        carried = lax.dot_general(
            out_maps, jnp.concatenate([high, low], axis=1), nt, preferred_element_type=f32
        )
        for i in range(heads):
            h = j * heads + i
            cols = slice(h * PH, (h + 1) * PH)
            inputs = x_ref[0, :, cols].astype(f32)
            gate = gate_ref[0, :, cols].astype(f32)
            y = kept[:, h : h + 1] * carried[:, i * PH : (i + 1) * PH]
            for s in range(drafts):
                y = y + mixing[s][:, h : h + 1] * inputs[s : s + 1]
            cols = slice(attended + h * PH, attended + (h + 1) * PH)
            mixed_ref[:, cols] = y * gate * jax.nn.sigmoid(gate)

    key_copy.wait()
    held = []
    for j in range(kv_heads):
        first = j * groups * head_size
        query = query_ref[0, :, first : first + groups * head_size].astype(f32)
        queries = jnp.concatenate(
            [query[:, g * head_size : (g + 1) * head_size] for g in range(groups)], axis=0
        )
        scores = lax.dot_general(
            queries.astype(bf16), keys_ref[:, j * head_size : (j + 1) * head_size], nt, preferred_element_type=f32
        ) * head_size ** (-0.5)
        position = lax.broadcasted_iota(jnp.int32, scores.shape, 1)
        scores = jnp.where(position < length_ref[...], scores, -jnp.inf)
        peak = jnp.max(scores, axis=1, keepdims=True)
        draft = lax.broadcasted_iota(jnp.int32, peak.shape, 0) % drafts
        new_cols = slice(j * head_size, (j + 1) * head_size)
        keys_new = key_new_ref[0, :, new_cols].astype(f32)
        scores_new = []
        for u in range(drafts):
            score = jnp.sum(queries * keys_new[u : u + 1, :], axis=1, keepdims=True)
            score = jnp.where(draft >= u, score * head_size ** (-0.5), -jnp.inf)
            scores_new.append(score)
            peak = jnp.maximum(peak, score)
        weights = jnp.exp(scores - peak)
        total = jnp.sum(weights, axis=1, keepdims=True)
        held.append((weights.astype(bf16), total, [jnp.exp(s - peak) for s in scores_new]))

    value_copy.wait()
    for j in range(kv_heads):
        first = j * groups * head_size
        new_cols = slice(j * head_size, (j + 1) * head_size)
        weights, total, weights_new = held[j]
        summed = jnp.dot(weights, values_ref[:, new_cols], preferred_element_type=f32)
        values_new = value_new_ref[0, :, new_cols].astype(f32)
        for u in range(drafts):
            weight = weights_new[u]
            total = total + weight
            summed = summed + weight.astype(bf16).astype(f32) * values_new[u : u + 1, :]
        result = summed / total
        for g in range(groups):
            cols = slice(first + g * head_size, first + (g + 1) * head_size)
            mixed_ref[:, cols] = result[g * drafts : (g + 1) * drafts]
    width = pieces_ref.shape[3]
    cols = pieces_ref.shape[1]
    for c in range(cols):
        piece = mixed_ref[:, c * width : (c + 1) * width].astype(bf16)
        for r in range(pieces_ref.shape[0]):
            pieces_ref[r, c] = piece


def mix(
    rows, cols, query, key_new, value_new, key_cache, value_cache, ctx_len,
    ssm_x, ssm_gate, ssm_b, ssm_c, ssm_dt, decay_rate, skip_gain, ssm_state,
):
    kv_heads = key_new.shape[2] // HD
    features = query.shape[2] + ssm_x.shape[2]
    ctx_len = ctx_len.reshape(1, 1)
    small = (
        ctx_len, query, key_new, value_new, ssm_x, ssm_gate, ssm_b, ssm_c, ssm_dt,
        decay_rate.reshape(1, -1), skip_gain.reshape(1, -1),
    )
    big = (key_cache, value_cache, ssm_state)
    cached = key_cache.shape[1:]
    return pl.pallas_call(
        mixer_kernel,
        in_specs=[pl.BlockSpec(memory_space=pltpu.HBM)] * (len(small) + len(big)),
        out_specs=pl.BlockSpec(memory_space=pltpu.VMEM),
        out_shape=jax.ShapeDtypeStruct(
            (rows, cols, query.shape[1], features // cols), jnp.bfloat16
        ),
        scratch_shapes=[pltpu.VMEM(array.shape, array.dtype) for array in small]
        + [
            pltpu.VMEM(cached, key_cache.dtype),
            pltpu.VMEM(cached, value_cache.dtype),
            pltpu.VMEM(ssm_state.shape[1:], ssm_state.dtype),
            pltpu.VMEM((query.shape[1], features), jnp.float32),
            pltpu.SemaphoreType.DMA((len(small),)),
            pltpu.SemaphoreType.DMA((3,)),
        ],
        compiler_params=pltpu.CompilerParams(vmem_limit_bytes=62 * 2**20),
        name="mixer",
    )(*small, *big)


def project_kernel(rows_ref, weights_ref, out_ref):
    out_ref[...] = jnp.dot(
        rows_ref[...], weights_ref[...], preferred_element_type=jnp.float32
    ).astype(out_ref.dtype)


def merge_kernel(rows_ref, weights_ref, part_ref, out_ref):
    product = jnp.dot(rows_ref[...], weights_ref[...], preferred_element_type=jnp.float32)
    out_ref[...] = (product + part_ref[...].astype(jnp.float32)).astype(out_ref.dtype)


def on_core(kernel, operands, out_shape, name, after=()):
    vmem = pl.BlockSpec(memory_space=pltpu.VMEM)
    count = len(operands)
    return pl.pallas_call(
        lambda *refs: kernel(*refs[:count], *refs[count + len(after) :]),
        in_specs=[vmem] * count + [pl.BlockSpec(memory_space=pl.ANY)] * len(after),
        out_specs=jax.tree.map(lambda _: vmem, out_shape),
        out_shape=out_shape,
        compiler_params=pltpu.CompilerParams(vmem_limit_bytes=16 * 2**20),
        name=name,
    )(*operands, *after)


def arrive_kernel(parts_ref, resid_ref, gain_ref, stream_ref, spread_ref):
    f32 = jnp.float32
    stream = resid_ref[...].astype(f32)
    for c in range(parts_ref.shape[0]):
        stream = stream + parts_ref[c].astype(f32)
    stream_ref[...] = stream
    scaled = (stream * gain_ref[...]).astype(spread_ref.dtype)
    for c in range(spread_ref.shape[0]):
        spread_ref[c] = scaled


def widen_kernel(rows, places, gain_ref, *refs):
    f32 = jnp.float32
    bf16 = jnp.bfloat16
    tokens, weights = refs[:rows], refs[rows : rows + len(places)]
    outs, ordered_ref = refs[rows + len(places) : -1], refs[-1]
    row = lax.axis_index("row")
    share = outs[0].shape[0]
    for q in range(rows):
        first = pl.multiple_of(lax.rem(q + rows - row, rows) * share, share)
        ordered_ref[pl.ds(first, share)] = tokens[q][...]
    for place, weight in zip(places, weights):
        units = weight.shape[0]
        sums = lax.dot_general(
            ordered_ref[...], weight[...], (((1,), (1,)), ((), ())), preferred_element_type=f32
        )
        if place + units == sum(w.shape[0] for w in weights):
            inverse = 1.0 / gain_ref[...]
            plain = ordered_ref[...].astype(f32) * inverse
            squares = jnp.sum(plain * plain, axis=1, keepdims=True)
            high = squares.astype(bf16).astype(f32)
            past = outs[0].shape[1] - (place + units)
            lane = lax.broadcasted_iota(jnp.int32, (squares.shape[0], past), 1)
            tail = jnp.where(lane == 0, high, jnp.where(lane == 1, squares - high, 0.0))
            sums = jnp.concatenate([sums, tail], axis=1)
        sums = sums.astype(bf16)
        for d in range(rows):
            outs[d][:, place : place + sums.shape[1]] = sums[d * share : (d + 1) * share]


def widen(tokens, gain, weights, places, rows):
    units = sum(weight.shape[0] for weight in weights)
    width = (units // 128 + 1) * 128
    share, depth = tokens[0].shape
    vmem = pl.BlockSpec(memory_space=pltpu.VMEM)
    return pl.pallas_call(
        functools.partial(widen_kernel, rows, places),
        in_specs=[vmem] * (1 + rows + len(weights)),
        out_specs=[vmem] * rows,
        out_shape=[jax.ShapeDtypeStruct((share, width), jnp.bfloat16)] * rows,
        scratch_shapes=[pltpu.VMEM((rows * share, depth), jnp.bfloat16)],
        compiler_params=pltpu.CompilerParams(vmem_limit_bytes=16 * 2**20),
        name="widen",
    )(gain, *tokens, *weights)


def gate_kernel(units, *refs):
    f32 = jnp.float32
    parts, out_ref = refs[:-1], refs[-1]
    summed = parts[0][...].astype(f32)
    for part in parts[1:]:
        summed = summed + part[...].astype(f32)
    squares = summed[:, 4 * units : 4 * units + 1] + summed[:, 4 * units + 1 : 4 * units + 2]
    summed = summed * lax.rsqrt(squares / D + norm_eps)
    hidden = []
    for first in (0, 2 * units):
        gate = summed[:, first : first + units]
        up = summed[:, first + units : first + 2 * units]
        hidden.append(gate * jax.nn.sigmoid(gate) * up)
    blank = jnp.zeros((summed.shape[0], out_ref.shape[1] - 2 * units), f32)
    hidden = jnp.concatenate([hidden[0], blank, hidden[1]], axis=1)
    out_ref[...] = hidden.astype(out_ref.dtype)


def add_kernel(*refs):
    total = refs[0][...].astype(jnp.float32)
    for ref in refs[1:-1]:
        total = total + ref[...].astype(jnp.float32)
    refs[-1][...] = total.astype(refs[-1].dtype)


def finish_kernel(parts_ref, stream_ref, out_ref):
    total = stream_ref[...]
    for c in range(parts_ref.shape[0]):
        total = total + parts_ref[c].astype(jnp.float32)
    out_ref[...] = total.astype(out_ref.dtype)


def narrow_kernel(rows, places, *refs):
    hidden_refs, weights = refs[:rows], refs[rows : rows + len(places)]
    outs, ordered_ref = refs[rows + len(places) : -1], refs[-1]
    row = lax.axis_index("row")
    share = hidden_refs[0].shape[0]
    for d in range(rows):
        first = pl.multiple_of(lax.rem(row + rows - d, rows) * share, share)
        ordered_ref[pl.ds(first, share)] = hidden_refs[d][...]
    down = None
    for place, weight in zip(places, weights):
        part = jnp.dot(
            ordered_ref[:, place : place + weight.shape[0]],
            weight[...],
            preferred_element_type=jnp.float32,
        )
        down = part if down is None else down + part
    down = down.astype(outs[0].dtype)
    for d in range(rows):
        outs[d][...] = down[d * share : (d + 1) * share]


def narrow(hidden, weights, places):
    rows = len(hidden)
    share, units = hidden[0].shape
    vmem = pl.BlockSpec(memory_space=pltpu.VMEM)
    return pl.pallas_call(
        functools.partial(narrow_kernel, rows, places),
        in_specs=[vmem] * (rows + len(weights)),
        out_specs=[vmem] * rows,
        out_shape=[jax.ShapeDtypeStruct((share, weights[0].shape[1]), jnp.bfloat16)] * rows,
        scratch_shapes=[pltpu.VMEM((rows * share, units), jnp.bfloat16)],
        compiler_params=pltpu.CompilerParams(vmem_limit_bytes=16 * 2**20),
        name="narrow",
    )(*hidden, *weights)


def state_kernel(accepted_ref, x_ref, in_map_ref, dt_ref, rate_ref, state_ref, *refs):
    f32 = jnp.float32
    out_ref = refs[-1]
    heads = state_ref.shape[1]
    dt = dt_ref[0]
    drafts = dt.shape[0]
    row = lax.broadcasted_iota(jnp.int32, dt.shape, 0)
    lane = lax.broadcasted_iota(jnp.int32, dt.shape, 1)
    taken = row < accepted_ref[0]
    step = jnp.where(taken, dt, 0.0) * rate_ref[...]
    after = [jnp.zeros_like(step[:1])]
    for t in range(drafts - 1, 0, -1):
        after.insert(0, after[0] + step[t : t + 1])
    whole = jnp.exp(-(after[0] + step[:1]))
    share = jnp.where(taken, jnp.exp(-jnp.concatenate(after, axis=0)) * dt, 0.0)
    terms = []
    for i in range(heads):
        mine = lane == pl.program_id(0) * heads + i
        part = jnp.sum(jnp.where(mine, share, 0.0), axis=1, keepdims=True)
        terms.append(part * x_ref[0, :, i * PH : (i + 1) * PH].astype(f32))
    added = lax.dot_general(
        jnp.concatenate(terms, axis=1),
        in_map_ref[0].astype(f32),
        (((0,), (0,)), ((), ())),
        precision=lax.Precision.HIGHEST,
        preferred_element_type=f32,
    )
    for i in range(heads):
        mine = lane[:1] == pl.program_id(0) * heads + i
        keep = jnp.sum(jnp.where(mine, whole, 0.0), axis=1, keepdims=True)
        out_ref[0, i] = keep * state_ref[0, i] + added[i * PH : (i + 1) * PH]


def final_state(ssm_x, ssm_b, ssm_dt, decay_rate, ssm_state, accepted, after):
    steps = 4
    heads = ssm_state.shape[1] // steps

    def whole(array):
        return pl.BlockSpec(array.shape, lambda j: (0,) * array.ndim)

    decay_rate = decay_rate.reshape(1, -1)
    block = pl.BlockSpec((1, heads) + ssm_state.shape[2:], lambda j: (0, j, 0, 0))
    return pl.pallas_call(
        state_kernel,
        grid=(steps,),
        in_specs=[
            pl.BlockSpec(memory_space=pltpu.SMEM),
            pl.BlockSpec(ssm_x.shape[:2] + (heads * PH,), lambda j: (0, 0, j)),
            whole(ssm_b),
            whole(ssm_dt),
            whole(decay_rate),
            block,
            pl.BlockSpec(memory_space=pl.ANY),
        ],
        out_specs=block,
        out_shape=jax.ShapeDtypeStruct(ssm_state.shape, ssm_state.dtype),
        compiler_params=pltpu.CompilerParams(vmem_limit_bytes=16 * 2**20),
        name="final_state",
    )(accepted, ssm_x, ssm_b, ssm_dt, decay_rate, ssm_state, after)


def exchange(blocks, axis, groups=None):
    return lax.all_to_all(blocks, axis, 0, 0, tiled=True, axis_index_groups=groups)


def shifted(blocks, axis):
    size = lax.axis_size(axis)
    return [blocks[0]] + [
        lax.ppermute(blocks[shift], axis, [(k, (k + shift) % size) for k in range(size)])
        for shift in range(1, size)
    ]


def around(blocks, size, sign):
    outer = lax.axis_size("col") // size
    return [blocks[0]] + [
        lax.ppermute(
            blocks[shift],
            "col",
            [
                (o * size + i, o * size + (i + sign * shift) % size)
                for o in range(outer)
                for i in range(size)
            ],
        )
        for shift in range(1, size)
    ]


def from_partner(weights):
    return lax.ppermute(weights, "grp", [(0, 1), (1, 0)])


def shards(
    resid,
    query,
    key_new,
    value_new,
    key_cache,
    value_cache,
    ctx_len,
    ssm_x,
    ssm_gate,
    ssm_b,
    ssm_c,
    ssm_dt,
    decay_rate,
    skip_gain,
    ssm_state,
    accepted,
    slot_of,
    w_out,
    norm_gain,
    gate_up,
    w_down,
):
    f32 = jnp.float32
    bf16 = jnp.bfloat16
    rows = lax.axis_size("row")
    cols = lax.axis_size("col")
    steps_new = query.shape[1]
    inner = 4
    lines = [[o * inner + i for o in range(cols // inner)] for i in range(inner)]
    pieces = mix(
        rows, cols, query, key_new, value_new, key_cache, value_cache, ctx_len,
        ssm_x, ssm_gate, ssm_b, ssm_c, ssm_dt, decay_rate, skip_gain, ssm_state,
    )
    width = pieces.shape[3]
    by_slot = exchange(pieces.reshape((rows * cols,) + pieces.shape[2:]), ("row", "col"))
    place = slot_of.reshape(2, -1)
    place = jnp.where(lax.axis_index("grp") == 1, place, place[::-1])
    for_other = jnp.take(by_slot, place[0], axis=0).reshape(-1, width)
    own = jnp.take(by_slot, place[1], axis=0).reshape(-1, width)
    held = jax.ShapeDtypeStruct((own.shape[0], w_out.shape[1]), bf16)
    for_other = on_core(project_kernel, (for_other, w_out), held, "project")
    half = on_core(merge_kernel, (own, w_out, from_partner(for_other)), held, "merge")
    half, gate_up, w_down, gain = lax.optimization_barrier((half, gate_up, w_down, norm_gain))
    state_next = final_state(ssm_x, ssm_b, ssm_dt, decay_rate, ssm_state, accepted, half)
    half = exchange(half.reshape(cols, -1, half.shape[1]), "col")
    units = gate_up.shape[2]
    in_weights = jnp.transpose(gate_up, (1, 2, 0)).reshape(2 * units, -1)
    in_pieces = [from_partner(in_weights), in_weights]
    in_places = [0, 2 * units]
    down_pieces = [from_partner(w_down), w_down]
    padded = -(-units // 128) * 128
    down_places = [0, padded]
    gain = gain.reshape(1, -1)
    stream, spread = on_core(
        arrive_kernel,
        (half, resid, gain),
        [
            jax.ShapeDtypeStruct(resid.shape, f32),
            jax.ShapeDtypeStruct((cols // inner,) + resid.shape, bf16),
        ],
        "arrive",
        [piece[:16, :128] for piece in in_pieces[:-1] + down_pieces[:-1]],
    )
    spread = exchange(spread, "col", lines)
    tokens = [
        block.reshape(-1, block.shape[2]) for block in around([spread] * inner, inner, 1)
    ]
    sums = shifted(widen(tokens, gain, in_pieces, in_places, rows), "row")
    held = jax.ShapeDtypeStruct((sums[0].shape[0], padded + units), bf16)
    hidden = on_core(functools.partial(gate_kernel, units), sums, held, "gate")
    down = narrow(shifted([hidden] * rows, "row"), down_pieces, down_places)
    down = around(down, inner, -1)
    held = jax.ShapeDtypeStruct(down[0].shape, bf16)
    down = on_core(add_kernel, down, held, "add")
    down = exchange(down.reshape(cols // inner, -1, down.shape[1]), "col", lines)
    held = jax.ShapeDtypeStruct(stream.shape, bf16)
    layer_out = on_core(finish_kernel, (down, stream), held, "finish")
    return (layer_out, state_next)


def solution(mesh):
    placed = (
        P(("grp", "col"), "row"),
        P(("row", "col"), None, "grp"),
        P(("row", "col"), None, "grp"),
        P(("row", "col"), None, "grp"),
        P(("row", "col"), None, "grp"),
        P(("row", "col"), None, "grp"),
        P(("row", "col")),
        P(("row", "col"), None, "grp"),
        P(("row", "col"), None, "grp"),
        P(("row", "col"), None, None),
        P(("row", "col"), None, None),
        P(("row", "col"), None, "grp"),
        P("grp"),
        P("grp"),
        P(("row", "col"), "grp", None, None),
        P(("row", "col")),
        P(),
        P(("grp", "col"), "row"),
        P("row"),
        P("row", None, ("grp", "col")),
        P(("grp", "col"), "row"),
    )
    return jax.shard_map(
        shards,
        mesh=mesh,
        in_specs=placed,
        out_specs=(P(("grp", "col"), "row"), P(("row", "col"), "grp", None, None)),
        check_vma=False,
    )
```
